32 devices in a mesh: group: 4 (over x, core), fsdp: 8 (over z, y).
Axes of the slice: x: 2, y: 2, z: 4, core: 2. Of those that a mesh axis runs over, the one named last changes fastest.
Arguments:
- tokens: bfloat16 [16384, 3072], P(('group', 'fsdp')), may hold values from -6 to 6
- student: float32 [4, 3072, 6144], P('group', 'fsdp'), may hold values from -6 to 6
- teacher: float32 [3072, 6144], P('fsdp', 'group'), may hold values from -6 to 6
- norm_gain: float32 [3072], replicated, may hold values from 0.5 to 1.5
- query_gain: float32 [128], replicated, may hold values from 0.5 to 1.5
- key_gain: float32 [128], replicated, may hold values from 0.5 to 1.5
Outputs:
- teacher_new: float32 [3072, 6144], P('fsdp', 'group')
- student_new: float32 [3072, 6144], P('fsdp', 'group')
- query: bfloat16 [16384, 3072], P(('group', 'fsdp'))
- key: bfloat16 [16384, 3072], P(('group', 'fsdp'))
The draws below stay inside these ranges and needn't reach their ends.
All inputs are finite; a program needn't handle non-finite values.
Results may differ from the reference program's by a relative error of at most 0.0058.
Values may be sent and summed in bfloat16 or wider, within the bound.
A program may use at most 192 MiB of HBM per device.

```python
import jax
import jax.numpy as jnp
from jax import lax

D = 3072
HEAD = 128
TOK_DEV = 512
GROUPS = 4
TOKENS = 16384
N_GROUP = 4
N_FSDP = 8


def raised(result, rng, source, target, blocks, factor):
    owner, partner = [(jnp.arange(result.shape[axis_at]) // (result.shape[axis_at] // blocks)).reshape([-1 if axis == axis_at else 1 for axis in range(result.ndim)]) for axis_at in (source, target)]
    chosen = jax.random.permutation(rng, blocks)[partner]
    strong = (owner == chosen) | (owner == (partner + blocks // 2) % blocks)
    return jnp.where(strong, factor * result, result)


def shard_levels(own_key, dims, shards, least, top_value):
    def one(position, blocks):
        draws = jax.random.uniform(jax.random.fold_in(jax.random.fold_in(own_key, 6), position), (blocks,), jnp.float32, least / len(shards), top_value / len(shards))
        return jnp.repeat(jnp.exp(draws), dims[position] // blocks).reshape((-1,) + (1,) * (len(dims) - position - 1))

    factor_of = one(*shards[0])
    for cut in shards[1:]:
        factor_of = factor_of * one(*cut)
    return factor_of


def noise(stream_key, extent, scale, most, shards=(), dtype=jnp.bfloat16):
    values = jax.random.normal(stream_key, extent, jnp.float32) * scale
    if len(shards) > 0:
        values = shard_levels(stream_key, extent, shards, -0.22, 0.18) * values
    return jnp.clip(values, min=-most, max=most).astype(dtype)


def heavy_noise(stream_key, shape, scale, bound, pieces, heavy, held_as=jnp.bfloat16):
    entries = scale * jax.random.normal(stream_key, shape, jnp.float32)
    if pieces:
        entries = entries * shard_levels(stream_key, shape, pieces, -0.22, 0.18)
    return jnp.clip(raised(entries, jax.random.fold_in(stream_key, 3), *heavy), -bound, bound).astype(held_as)


def setup_inputs(seed: int = 0) -> dict:
    key_list = jax.random.split(jax.random.key(seed), 7)
    tokens = noise(key_list[0], (TOKENS, D), 1.0, 6.0, ((0, 32),))
    student = heavy_noise(key_list[1], (GROUPS, D, 2 * D), 1.0, 6.0, ((0, 4), (1, 8)), (0, 2, 4, 2.0), jnp.float32)
    teacher = noise(key_list[2], (D, 2 * D), 1.0, 6.0, ((0, 8), (1, 4)), jnp.float32)
    norm_gain = jnp.clip(1.0 + 0.1 * jax.random.normal(key_list[3], (D,), jnp.float32), 0.5, 1.5)
    query_gain = jnp.clip(1.0 + 0.1 * jax.random.normal(key_list[4], (HEAD,), jnp.float32), 0.5, 1.5)
    key_gain = jnp.clip(1.0 + 0.1 * jax.random.normal(key_list[5], (HEAD,), jnp.float32), 0.5, 1.5)
    return dict(tokens=tokens, student=student, teacher=teacher, norm_gain=norm_gain, query_gain=query_gain, key_gain=key_gain)


ema_decay = 0.99

def head_norm(values, gain):
    shaped = values.reshape(values.shape[0], D // HEAD, HEAD)
    scaled = shaped * lax.rsqrt(lax.optimization_barrier(jnp.mean(shaped * shaped, axis=-1, keepdims=True)) + 1e-06) * gain
    return scaled.reshape(values.shape[0], D).astype(jnp.bfloat16)

def reference(tokens, student, teacher, norm_gain, query_gain, key_gain):
    student_new = lax.optimization_barrier(jnp.sum(student, axis=0)) / N_GROUP
    teacher_new = ema_decay * teacher + (1.0 - ema_decay) * student_new
    copied = student_new.astype(jnp.bfloat16)
    blocks = tokens.reshape(N_GROUP * N_FSDP, TOK_DEV, D)

    def one_block(block):
        wide = block.astype(jnp.float32)
        normed = (wide * lax.rsqrt(lax.optimization_barrier(jnp.mean(wide * wide, axis=-1, keepdims=True)) + 1e-06) * norm_gain).astype(jnp.bfloat16)
        projected = jnp.dot(normed, copied, preferred_element_type=jnp.float32) * D ** (-0.5)
        return (head_norm(projected[:, :D], query_gain), head_norm(projected[:, D:], key_gain))
    query, key = lax.map(one_block, blocks)
    return (teacher_new, student_new, query.reshape(TOKENS, D), key.reshape(TOKENS, D))
```

```python
import functools

import jax
import jax.numpy as jnp
from jax import lax
from jax.experimental import pallas as pl
from jax.experimental.pallas import tpu as pltpu
from jax.sharding import PartitionSpec as P

HEAD = 128
PAIR = 2
EMA_DECAY = 0.99
MESH = pl.DeviceIdType.MESH
ROUTES = ("yx", "xy", "xy")


def chunk_count(width, line):
    heads = width // HEAD
    most = max(1, 24 // line)
    return max(n for n in range(1, heads + 1) if heads % n == 0 and n <= most)


def kernel(
    groups,
    line,
    chunks,
    student,
    tokens,
    teacher,
    norm_gain,
    query_gain,
    key_gain,
    teacher_new,
    student_new,
    query,
    key,
    own_part,
    core_part,
    pair_out,
    pair_in,
    weights,
    normed,
    staged,
    mean_out,
    teacher_out,
    load_sem,
    core_send,
    core_recv,
    pair_send,
    pair_recv,
    line_send,
    line_recv,
    first_send,
    first_recv,
    last_send,
    last_recv,
    token_sem,
    store_sem,
    keep_sem,
    give_send,
    give_recv,
):
    g = lax.axis_index("group")
    f = lax.axis_index("fsdp")
    x, c = g // PAIR, g % PAIR
    z, y = f // PAIR, f % PAIR
    rows, block = mean_out.shape[1], mean_out.shape[2]
    width = block * chunks
    per_token, model_width = tokens.shape
    mate = (x * PAIR + 1 - c, f)
    across = ((1 - x) * PAIR + c, f)
    beside = (g, z * PAIR + 1 - y)
    below = (g, (z - 1) * PAIR + y)
    above = (g, (z + 1) * PAIR + y)

    barrier = pltpu.get_barrier_semaphore()
    for device in (mate, across, beside):
        pl.semaphore_signal(barrier, inc=1, device_id=device, device_id_type=MESH)

    @pl.when(z > 0)
    def _():
        pl.semaphore_signal(barrier, inc=1, device_id=below, device_id_type=MESH)

    @pl.when(z < line - 1)
    def _():
        pl.semaphore_signal(barrier, inc=1, device_id=above, device_id_type=MESH)

    peers = 3 + jnp.where(z > 0, 1, 0) + jnp.where(z < line - 1, 1, 0)
    pl.semaphore_wait(barrier, peers)

    def remote(src, dst, send, recv, device):
        return pltpu.make_async_remote_copy(
            src_ref=src, dst_ref=dst, send_sem=send, recv_sem=recv, device_id=device, device_id_type=MESH
        )

    def columns(half, core, k):
        start = half * (PAIR * width) + core * width + k * block
        return pl.ds(pl.multiple_of(start, HEAD), block)

    def load(k, half):
        return pltpu.make_async_copy(
            student.at[0, :, columns(half, c, k)], own_part.at[k, half], load_sem.at[k, half]
        )

    def to_mate(k, half):
        return remote(
            student.at[0, :, columns(half, 1 - c, k)],
            core_part.at[k, half],
            core_send.at[k, half],
            core_recv.at[k, half],
            mate,
        )

    def to_across(k):
        return remote(pair_out.at[k], pair_in.at[k], pair_send.at[k], pair_recv.at[k], across)

    def shard(k, half, index, count=1):
        span = pl.ds(pl.multiple_of(index * rows, 16), count * rows)
        return weights.at[k, half, span, :]

    def along(k, slab, way):
        part = shard(k, x, slab * PAIR + y)
        return remote(
            part, part, line_send.at[k, way, slab], line_recv.at[k, slab], (below, above)[way]
        )

    def first(k, slab):
        part = shard(k, x, slab * PAIR + y)
        device = across if ROUTES[k % len(ROUTES)] == "xy" else beside
        return remote(part, part, first_send.at[k, slab], first_recv.at[k, slab], device)

    def last(k, slab):
        if ROUTES[k % len(ROUTES)] == "xy":
            span = pl.ds(pl.multiple_of((slab * PAIR + y) * rows, 16), rows)
            part, device = weights.at[k, :, span, :], beside
        else:
            part, device = shard(k, x, slab * PAIR, PAIR), across
        return remote(part, part, last_send.at[k, slab], last_recv.at[k, slab], device)

    def tokens_to_mate():
        return remote(normed.at[c], normed.at[c], token_sem.at[0], token_sem.at[1], mate)

    def stores(k):
        here = pl.ds(k * block, block)
        return (
            pltpu.make_async_copy(mean_out.at[k], student_new.at[:, here], store_sem.at[k, 0]),
            pltpu.make_async_copy(teacher_out.at[k], teacher_new.at[:, here], store_sem.at[k, 1]),
        )

    def out_columns(k):
        return pl.ds(pl.multiple_of(c * width + k * block, HEAD), block)

    def keep(k, half):
        out = (query, key)[half]
        return pltpu.make_async_copy(
            staged.at[k, half, c], out.at[:, out_columns(k)], keep_sem.at[k, half]
        )

    def give(k, half):
        out = (query, key)[half]
        return remote(
            staged.at[k, half, 1 - c],
            out.at[:, out_columns(k)],
            give_send.at[k, half],
            give_recv.at[k, half],
            mate,
        )

    def norm_tokens():
        step = 64

        def body(i, carry):
            at = pl.ds(pl.multiple_of(i * step, step), step)
            wide = tokens[at, :].astype(jnp.float32)
            scale = lax.rsqrt(jnp.mean(wide * wide, axis=-1, keepdims=True) + 1e-06)
            normed[c, at, :] = (wide * scale * norm_gain[...]).astype(jnp.bfloat16)
            return carry

        lax.fori_loop(0, per_token // step, body, 0)
        tokens_to_mate().start()

    def sum_cores(k):
        for half in range(PAIR):
            load(k, half).wait()
            to_mate(k, half).wait_recv()
        pair_out[k] = (own_part[k, 1 - x] + core_part[k, 1 - x]).astype(jnp.bfloat16)
        to_across(k).start()

    def sum_pair(k):
        to_across(k).wait_recv()
        total = (own_part[k, x] + core_part[k, x] + pair_in[k].astype(jnp.float32)) / groups
        mean_out[k] = total
        here = pl.ds(k * block, block)
        teacher_out[k] = EMA_DECAY * teacher[:, here] + (1.0 - EMA_DECAY) * total
        weights[k, x, pl.ds(pl.multiple_of(f * rows, 16), rows), :] = total.astype(jnp.bfloat16)

        @pl.when(z > 0)
        def _():
            along(k, z, 0).start()

        @pl.when(z < line - 1)
        def _():
            along(k, z, 1).start()

        first(k, z).start()
        for copy in stores(k):
            copy.start()

    def sides(t):
        yield z >= t, z - t, 1, z < line - 1
        yield z < line - t, z + t, 0, z > 0

    def line_step(k, t):
        for there, slab, way, onward in sides(t):

            @pl.when(there)
            def _():
                along(k, slab, way).wait_recv()

                @pl.when(onward)
                def _():
                    along(k, slab, way).start()

                first(k, slab).start()

    def plane_step(k, t):
        if t == 0:
            first(k, z).wait_recv()
            last(k, z).start()
            return
        for there, slab, way, onward in sides(t):

            @pl.when(there)
            def _():
                first(k, slab).wait_recv()
                last(k, slab).start()

    def arrived(k):
        for slab in range(line):
            last(k, slab).wait_recv()

    def project(k, half, core):
        step = 256 if per_token % 256 == 0 else per_token
        tile = 256 if block % 256 == 0 else HEAD
        gain = (query_gain, key_gain)[half][...]

        def body(i, carry):
            at = pl.ds(pl.multiple_of(i * step, step), step)
            for start in range(0, block, tile):
                made = jnp.dot(
                    normed[core, at, :],
                    weights[k, half, :, start : start + tile],
                    preferred_element_type=jnp.float32,
                )
                made = made * model_width ** (-0.5)
                for head in range(0, tile, HEAD):
                    one = made[:, head : head + HEAD]
                    scale = lax.rsqrt(jnp.mean(one * one, axis=-1, keepdims=True) + 1e-06)
                    staged[k, half, core, at, start + head : start + head + HEAD] = (
                        one * scale * gain
                    ).astype(jnp.bfloat16)
            return carry

        lax.fori_loop(0, per_token // step, body, 0)

    def project_other(k, half):
        project(k, half, 1 - c)
        give(k, half).start()

    def project_own(k, half):
        project(k, half, c)
        keep(k, half).start()

    for k in range(chunks):
        for half in range(PAIR):
            to_mate(k, half).start()
            load(k, half).start()
    norm_tokens()

    events = []
    period, hop = 25, 4
    for k in range(chunks):
        events.append((4 + k, functools.partial(sum_cores, k)))
        events.append((12 + 4 * k, functools.partial(sum_pair, k)))
        for t in range(1, line):
            events.append((12 + 12 * k + hop * t, functools.partial(line_step, k, t)))
        for t in range(line):
            events.append((20 + period * k + 6 * t, functools.partial(plane_step, k, t)))
        done = 30 + period * (k + 1)
        events.append((done, functools.partial(arrived, k)))
        if k == 0:
            events.append((done, lambda: tokens_to_mate().wait_recv()))
        for half in range(PAIR):
            events.append((done + 6 * half, functools.partial(project_other, k, half)))
            events.append((done + 6 * half + 3, functools.partial(project_own, k, half)))
    for _, event in sorted(events, key=lambda item: item[0]):
        event()

    tokens_to_mate().wait_send()
    for k in range(chunks):
        to_across(k).wait_send()
        for half in range(PAIR):
            to_mate(k, half).wait_send()
            keep(k, half).wait()
            give(k, half).wait_send()
        for copy in stores(k):
            copy.wait()
        for slab in range(line):
            first(k, slab).wait_send()
            last(k, slab).wait_send()

            @pl.when((z > 0) & (z <= slab))
            def _():
                along(k, slab, 0).wait_send()

            @pl.when((z < line - 1) & (z >= slab))
            def _():
                along(k, slab, 1).wait_send()

    for k in range(chunks):
        for half in range(PAIR):
            give(k, half).wait_recv()


def shards(groups, members, tokens, student, teacher, norm_gain, query_gain, key_gain):
    per_token, model_width = tokens.shape
    rows, width = teacher.shape
    line = members // PAIR
    chunks = chunk_count(width, line)
    block = width // chunks
    dma = pltpu.SemaphoreType.DMA
    vmem = pl.BlockSpec(memory_space=pltpu.VMEM)
    hbm = pl.BlockSpec(memory_space=pl.ANY)
    f32, bf16 = jnp.float32, jnp.bfloat16
    return pl.pallas_call(
        functools.partial(kernel, groups, line, chunks),
        out_shape=(
            jax.ShapeDtypeStruct((rows, width), f32),
            jax.ShapeDtypeStruct((rows, width), f32),
            jax.ShapeDtypeStruct((per_token, model_width), bf16),
            jax.ShapeDtypeStruct((per_token, model_width), bf16),
        ),
        in_specs=[hbm, vmem, vmem, vmem, vmem, vmem],
        out_specs=(hbm, hbm, hbm, hbm),
        scratch_shapes=[
            pltpu.VMEM((chunks, PAIR, rows, block), f32),
            pltpu.VMEM((chunks, PAIR, rows, block), f32),
            pltpu.VMEM((chunks, rows, block), bf16),
            pltpu.VMEM((chunks, rows, block), bf16),
            pltpu.VMEM((chunks, PAIR, rows * members, block), bf16),
            pltpu.VMEM((PAIR, per_token, model_width), bf16),
            pltpu.VMEM((chunks, PAIR, PAIR, per_token, block), bf16),
            pltpu.VMEM((chunks, rows, block), f32),
            pltpu.VMEM((chunks, rows, block), f32),
            dma((chunks, PAIR)),
            dma((chunks, PAIR)),
            dma((chunks, PAIR)),
            dma((chunks,)),
            dma((chunks,)),
            dma((chunks, 2, line)),
            dma((chunks, line)),
            dma((chunks, line)),
            dma((chunks, line)),
            dma((chunks, line)),
            dma((chunks, line)),
            dma((2,)),
            dma((chunks, 2)),
            dma((chunks, PAIR)),
            dma((chunks, PAIR)),
            dma((chunks, PAIR)),
        ],
        compiler_params=pltpu.CompilerParams(
            collective_id=0, has_side_effects=True, vmem_limit_bytes=60 * 2**20
        ),
        cost_estimate=pl.CostEstimate(
            flops=4 * per_token * model_width * model_width,
            bytes_accessed=4 * student.size + 8 * tokens.size,
            transcendentals=0,
        ),
    )(
        student,
        tokens,
        teacher,
        norm_gain.reshape(1, -1),
        query_gain.reshape(1, -1),
        key_gain.reshape(1, -1),
    )


def solution(mesh):
    placed = (
        P(("group", "fsdp"), None),
        P("group", "fsdp", None),
        P("fsdp", "group"),
        P(),
        P(),
        P(),
    )
    return jax.shard_map(
        functools.partial(shards, mesh.shape["group"], mesh.shape["fsdp"]),
        mesh=mesh,
        in_specs=placed,
        out_specs=(
            P("fsdp", "group"),
            P("fsdp", "group"),
            P(("group", "fsdp"), None),
            P(("group", "fsdp"), None),
        ),
        check_vma=False,
    )
```

```python
import functools

import jax
import jax.numpy as jnp
from jax import lax
from jax.experimental import pallas as pl
from jax.experimental.pallas import tpu as pltpu
from jax.sharding import PartitionSpec as P

HEAD = 128
PAIR = 2
EMA_DECAY = 0.99
MESH = pl.DeviceIdType.MESH
ROUTES = ("yx", "xy", "xy")


def chunk_count(width, line):
    heads = width // HEAD
    most = max(1, 24 // line)
    return max(n for n in range(1, heads + 1) if heads % n == 0 and n <= most)


def kernel(
    groups,
    line,
    chunks,
    student,
    tokens,
    teacher,
    norm_gain,
    query_gain,
    key_gain,
    teacher_new,
    student_new,
    query,
    key,
    own_part,
    core_part,
    pair_out,
    pair_in,
    weights,
    normed,
    staged,
    mean_out,
    teacher_out,
    load_sem,
    core_send,
    core_recv,
    pair_send,
    pair_recv,
    line_send,
    line_recv,
    first_send,
    first_recv,
    last_send,
    last_recv,
    token_sem,
    store_sem,
    keep_sem,
    give_send,
    give_recv,
):
    g = lax.axis_index("group")
    f = lax.axis_index("fsdp")
    x, c = g // PAIR, g % PAIR
    z, y = f // PAIR, f % PAIR
    rows, block = mean_out.shape[1], mean_out.shape[2]
    width = block * chunks
    per_token, model_width = tokens.shape
    mate = (x * PAIR + 1 - c, f)
    across = ((1 - x) * PAIR + c, f)
    beside = (g, z * PAIR + 1 - y)
    below = (g, (z - 1) * PAIR + y)
    above = (g, (z + 1) * PAIR + y)

    barrier = pltpu.get_barrier_semaphore()
    for device in (mate, across, beside):
        pl.semaphore_signal(barrier, inc=1, device_id=device, device_id_type=MESH)

    @pl.when(z > 0)
    def _():
        pl.semaphore_signal(barrier, inc=1, device_id=below, device_id_type=MESH)

    @pl.when(z < line - 1)
    def _():
        pl.semaphore_signal(barrier, inc=1, device_id=above, device_id_type=MESH)

    peers = 3 + jnp.where(z > 0, 1, 0) + jnp.where(z < line - 1, 1, 0)
    pl.semaphore_wait(barrier, peers)

    def remote(src, dst, send, recv, device):
        return pltpu.make_async_remote_copy(
            src_ref=src, dst_ref=dst, send_sem=send, recv_sem=recv, device_id=device, device_id_type=MESH
        )

    def columns(half, core, k):
        start = half * (PAIR * width) + core * width + k * block
        return pl.ds(pl.multiple_of(start, HEAD), block)

    def load(k, half):
        return pltpu.make_async_copy(
            student.at[0, :, columns(half, c, k)], own_part.at[k, half], load_sem.at[k, half]
        )

    def to_mate(k, half):
        return remote(
            student.at[0, :, columns(half, 1 - c, k)],
            core_part.at[k, half],
            core_send.at[k, half],
            core_recv.at[k, half],
            mate,
        )

    def to_across(k):
        return remote(pair_out.at[k], pair_in.at[k], pair_send.at[k], pair_recv.at[k], across)

    def shard(k, half, index, count=1):
        span = pl.ds(pl.multiple_of(index * rows, 16), count * rows)
        return weights.at[k, half, span, :]

    def along(k, slab, way):
        part = shard(k, x, slab * PAIR + y)
        return remote(
            part, part, line_send.at[k, way, slab], line_recv.at[k, slab], (below, above)[way]
        )

    def first(k, slab):
        part = shard(k, x, slab * PAIR + y)
        device = across if ROUTES[k % len(ROUTES)] == "xy" else beside
        return remote(part, part, first_send.at[k, slab], first_recv.at[k, slab], device)

    def last(k, slab):
        if ROUTES[k % len(ROUTES)] == "xy":
            span = pl.ds(pl.multiple_of((slab * PAIR + y) * rows, 16), rows)
            part, device = weights.at[k, :, span, :], beside
        else:
            part, device = shard(k, x, slab * PAIR, PAIR), across
        return remote(part, part, last_send.at[k, slab], last_recv.at[k, slab], device)

    def tokens_to_mate():
        return remote(normed.at[c], normed.at[c], token_sem.at[0], token_sem.at[1], mate)

    def stores(k):
        here = pl.ds(k * block, block)
        return (
            pltpu.make_async_copy(mean_out.at[k], student_new.at[:, here], store_sem.at[k, 0]),
            pltpu.make_async_copy(teacher_out.at[k], teacher_new.at[:, here], store_sem.at[k, 1]),
        )

    def out_columns(k):
        return pl.ds(pl.multiple_of(c * width + k * block, HEAD), block)

    def keep(k, half):
        out = (query, key)[half]
        return pltpu.make_async_copy(
            staged.at[k, half, c], out.at[:, out_columns(k)], keep_sem.at[k, half]
        )

    def give(k, half):
        out = (query, key)[half]
        return remote(
            staged.at[k, half, 1 - c],
            out.at[:, out_columns(k)],
            give_send.at[k, half],
            give_recv.at[k, half],
            mate,
        )

    def norm_tokens():
        step = 64

        def body(i, carry):
            at = pl.ds(pl.multiple_of(i * step, step), step)
            wide = tokens[at, :].astype(jnp.float32)
            scale = lax.rsqrt(jnp.mean(wide * wide, axis=-1, keepdims=True) + 1e-06)
            normed[c, at, :] = (wide * scale * norm_gain[...]).astype(jnp.bfloat16)
            return carry

        lax.fori_loop(0, per_token // step, body, 0)
        tokens_to_mate().start()

    def sum_cores(k):
        for half in range(PAIR):
            load(k, half).wait()
            to_mate(k, half).wait_recv()
        pair_out[k] = (own_part[k, 1 - x] + core_part[k, 1 - x]).astype(jnp.bfloat16)
        to_across(k).start()

    def sum_pair(k):
        to_across(k).wait_recv()
        total = (own_part[k, x] + core_part[k, x] + pair_in[k].astype(jnp.float32)) / groups
        mean_out[k] = total
        here = pl.ds(k * block, block)
        teacher_out[k] = EMA_DECAY * teacher[:, here] + (1.0 - EMA_DECAY) * total
        weights[k, x, pl.ds(pl.multiple_of(f * rows, 16), rows), :] = total.astype(jnp.bfloat16)

        @pl.when(z > 0)
        def _():
            along(k, z, 0).start()

        @pl.when(z < line - 1)
        def _():
            along(k, z, 1).start()

        first(k, z).start()
        for copy in stores(k):
            copy.start()

    def sides(t):
        yield z >= t, z - t, 1, z < line - 1
        yield z < line - t, z + t, 0, z > 0

    def line_step(k, t):
        for there, slab, way, onward in sides(t):

            @pl.when(there)
            def _():
                along(k, slab, way).wait_recv()

                @pl.when(onward)
                def _():
                    along(k, slab, way).start()

                first(k, slab).start()

    def plane_step(k, t):
        if t == 0:
            first(k, z).wait_recv()
            last(k, z).start()
            return
        for there, slab, way, onward in sides(t):

            @pl.when(there)
            def _():
                first(k, slab).wait_recv()
                last(k, slab).start()

    def arrived(k):
        for slab in range(line):
            last(k, slab).wait_recv()

    def project(k, half, core):
        step = 256 if per_token % 256 == 0 else per_token
        tile = 256 if block % 256 == 0 else HEAD
        gain = (query_gain, key_gain)[half][...]

        def body(i, carry):
            at = pl.ds(pl.multiple_of(i * step, step), step)
            for start in range(0, block, tile):
                made = jnp.dot(
                    normed[core, at, :],
                    weights[k, half, :, start : start + tile],
                    preferred_element_type=jnp.float32,
                )
                made = made * model_width ** (-0.5)
                for head in range(0, tile, HEAD):
                    one = made[:, head : head + HEAD]
                    scale = lax.rsqrt(jnp.mean(one * one, axis=-1, keepdims=True) + 1e-06)
                    staged[k, half, core, at, start + head : start + head + HEAD] = (
                        one * scale * gain
                    ).astype(jnp.bfloat16)
            return carry

        lax.fori_loop(0, per_token // step, body, 0)

    def project_other(k, half):
        project(k, half, 1 - c)
        give(k, half).start()

    def project_own(k, half):
        project(k, half, c)
        keep(k, half).start()

    for k in range(chunks):
        for half in range(PAIR):
            to_mate(k, half).start()
            load(k, half).start()
    norm_tokens()

    events = []
    period, hop = 25, 4
    for k in range(chunks):
        events.append((4 + k, functools.partial(sum_cores, k)))
        events.append((12 + 4 * k, functools.partial(sum_pair, k)))
        for t in range(1, line):
            events.append((12 + 12 * k + hop * t, functools.partial(line_step, k, t)))
        for t in range(line):
            events.append((20 + period * k + 6 * t, functools.partial(plane_step, k, t)))
        done = 44 + period * (k + 1)
        events.append((done, functools.partial(arrived, k)))
        if k == 0:
            events.append((done, lambda: tokens_to_mate().wait_recv()))
        for half in range(PAIR):
            events.append((done + 6 * half, functools.partial(project_other, k, half)))
            events.append((done + 6 * half + 3, functools.partial(project_own, k, half)))
    for _, event in sorted(events, key=lambda item: item[0]):
        event()

    tokens_to_mate().wait_send()
    for k in range(chunks):
        to_across(k).wait_send()
        for half in range(PAIR):
            to_mate(k, half).wait_send()
            keep(k, half).wait()
            give(k, half).wait_send()
        for copy in stores(k):
            copy.wait()
        for slab in range(line):
            first(k, slab).wait_send()
            last(k, slab).wait_send()

            @pl.when((z > 0) & (z <= slab))
            def _():
                along(k, slab, 0).wait_send()

            @pl.when((z < line - 1) & (z >= slab))
            def _():
                along(k, slab, 1).wait_send()

    for k in range(chunks):
        for half in range(PAIR):
            give(k, half).wait_recv()


def shards(groups, members, tokens, student, teacher, norm_gain, query_gain, key_gain):
    per_token, model_width = tokens.shape
    rows, width = teacher.shape
    line = members // PAIR
    chunks = chunk_count(width, line)
    block = width // chunks
    dma = pltpu.SemaphoreType.DMA
    vmem = pl.BlockSpec(memory_space=pltpu.VMEM)
    hbm = pl.BlockSpec(memory_space=pl.ANY)
    f32, bf16 = jnp.float32, jnp.bfloat16
    return pl.pallas_call(
        functools.partial(kernel, groups, line, chunks),
        out_shape=(
            jax.ShapeDtypeStruct((rows, width), f32),
            jax.ShapeDtypeStruct((rows, width), f32),
            jax.ShapeDtypeStruct((per_token, model_width), bf16),
            jax.ShapeDtypeStruct((per_token, model_width), bf16),
        ),
        in_specs=[hbm, vmem, vmem, vmem, vmem, vmem],
        out_specs=(hbm, hbm, hbm, hbm),
        scratch_shapes=[
            pltpu.VMEM((chunks, PAIR, rows, block), f32),
            pltpu.VMEM((chunks, PAIR, rows, block), f32),
            pltpu.VMEM((chunks, rows, block), bf16),
            pltpu.VMEM((chunks, rows, block), bf16),
            pltpu.VMEM((chunks, PAIR, rows * members, block), bf16),
            pltpu.VMEM((PAIR, per_token, model_width), bf16),
            pltpu.VMEM((chunks, PAIR, PAIR, per_token, block), bf16),
            pltpu.VMEM((chunks, rows, block), f32),
            pltpu.VMEM((chunks, rows, block), f32),
            dma((chunks, PAIR)),
            dma((chunks, PAIR)),
            dma((chunks, PAIR)),
            dma((chunks,)),
            dma((chunks,)),
            dma((chunks, 2, line)),
            dma((chunks, line)),
            dma((chunks, line)),
            dma((chunks, line)),
            dma((chunks, line)),
            dma((chunks, line)),
            dma((2,)),
            dma((chunks, 2)),
            dma((chunks, PAIR)),
            dma((chunks, PAIR)),
            dma((chunks, PAIR)),
        ],
        compiler_params=pltpu.CompilerParams(
            collective_id=0, has_side_effects=True, vmem_limit_bytes=60 * 2**20
        ),
        cost_estimate=pl.CostEstimate(
            flops=4 * per_token * model_width * model_width,
            bytes_accessed=4 * student.size + 8 * tokens.size,
            transcendentals=0,
        ),
    )(
        student,
        tokens,
        teacher,
        norm_gain.reshape(1, -1),
        query_gain.reshape(1, -1),
        key_gain.reshape(1, -1),
    )


def solution(mesh):
    placed = (
        P(("group", "fsdp"), None),
        P("group", "fsdp", None),
        P("fsdp", "group"),
        P(),
        P(),
        P(),
    )
    return jax.shard_map(
        functools.partial(shards, mesh.shape["group"], mesh.shape["fsdp"]),
        mesh=mesh,
        in_specs=placed,
        out_specs=(
            P("fsdp", "group"),
            P("fsdp", "group"),
            P(("group", "fsdp"), None),
            P(("group", "fsdp"), None),
        ),
        check_vma=False,
    )
```

```python
import functools

import jax
import jax.numpy as jnp
from jax import lax
from jax.experimental import pallas as pl
from jax.experimental.pallas import tpu as pltpu
from jax.sharding import PartitionSpec as P

HEAD = 128
PAIR = 2
EMA_DECAY = 0.99
MESH = pl.DeviceIdType.MESH
ROUTES = ("yx", "xy", "xy")


def chunk_count(width, line):
    heads = width // HEAD
    most = max(1, 24 // line)
    return max(n for n in range(1, heads + 1) if heads % n == 0 and n <= most)


def kernel(
    groups,
    line,
    chunks,
    student,
    tokens,
    teacher,
    norm_gain,
    query_gain,
    key_gain,
    teacher_new,
    student_new,
    query,
    key,
    own_part,
    core_part,
    pair_out,
    pair_in,
    weights,
    normed,
    staged,
    mean_out,
    teacher_out,
    load_sem,
    core_send,
    core_recv,
    pair_send,
    pair_recv,
    line_send,
    line_recv,
    first_send,
    first_recv,
    last_send,
    last_recv,
    token_sem,
    store_sem,
    keep_sem,
    give_send,
    give_recv,
):
    g = lax.axis_index("group")
    f = lax.axis_index("fsdp")
    x, c = g // PAIR, g % PAIR
    z, y = f // PAIR, f % PAIR
    rows, block = mean_out.shape[1], mean_out.shape[2]
    width = block * chunks
    per_token, model_width = tokens.shape
    mate = (x * PAIR + 1 - c, f)
    across = ((1 - x) * PAIR + c, f)
    beside = (g, z * PAIR + 1 - y)
    below = (g, (z - 1) * PAIR + y)
    above = (g, (z + 1) * PAIR + y)

    line_last = chunks - 1 if chunks > 2 else -1

    barrier = pltpu.get_barrier_semaphore()
    for device in (mate, across, beside):
        pl.semaphore_signal(barrier, inc=1, device_id=device, device_id_type=MESH)

    @pl.when(z > 0)
    def _():
        pl.semaphore_signal(barrier, inc=1, device_id=below, device_id_type=MESH)

    @pl.when(z < line - 1)
    def _():
        pl.semaphore_signal(barrier, inc=1, device_id=above, device_id_type=MESH)

    peers = 3 + jnp.where(z > 0, 1, 0) + jnp.where(z < line - 1, 1, 0)
    pl.semaphore_wait(barrier, peers)

    def remote(src, dst, send, recv, device):
        return pltpu.make_async_remote_copy(
            src_ref=src, dst_ref=dst, send_sem=send, recv_sem=recv, device_id=device, device_id_type=MESH
        )

    def columns(half, core, k):
        start = half * (PAIR * width) + core * width + k * block
        return pl.ds(pl.multiple_of(start, HEAD), block)

    def load(k, half):
        return pltpu.make_async_copy(
            student.at[0, :, columns(half, c, k)], own_part.at[k, half], load_sem.at[k, half]
        )

    def to_mate(k, half):
        return remote(
            student.at[0, :, columns(half, 1 - c, k)],
            core_part.at[k, half],
            core_send.at[k, half],
            core_recv.at[k, half],
            mate,
        )

    def to_across(k):
        return remote(pair_out.at[k], pair_in.at[k], pair_send.at[k], pair_recv.at[k], across)

    def shard(k, half, index, count=1):
        span = pl.ds(pl.multiple_of(index * rows, 16), count * rows)
        return weights.at[k, half, span, :]

    def along(k, slab, way):
        if k == line_last:
            span = pl.ds(pl.multiple_of(slab * PAIR * rows, 16), PAIR * rows)
            part = weights.at[k, :, span, :]
        else:
            part = shard(k, x, slab * PAIR + y)
        return remote(
            part, part, line_send.at[k, way, slab], line_recv.at[k, slab], (below, above)[way]
        )

    def first(k, slab):
        part = shard(k, x, slab * PAIR + y)
        device = across if ROUTES[k % len(ROUTES)] == "xy" else beside
        return remote(part, part, first_send.at[k, slab], first_recv.at[k, slab], device)

    def last(k, slab):
        if ROUTES[k % len(ROUTES)] == "xy":
            span = pl.ds(pl.multiple_of((slab * PAIR + y) * rows, 16), rows)
            part, device = weights.at[k, :, span, :], beside
        else:
            part, device = shard(k, x, slab * PAIR, PAIR), across
        return remote(part, part, last_send.at[k, slab], last_recv.at[k, slab], device)

    def tokens_to_mate():
        return remote(normed.at[c], normed.at[c], token_sem.at[0], token_sem.at[1], mate)

    def stores(k):
        here = pl.ds(k * block, block)
        return (
            pltpu.make_async_copy(mean_out.at[k], student_new.at[:, here], store_sem.at[k, 0]),
            pltpu.make_async_copy(teacher_out.at[k], teacher_new.at[:, here], store_sem.at[k, 1]),
        )

    def out_columns(k):
        return pl.ds(pl.multiple_of(c * width + k * block, HEAD), block)

    def keep(k, half):
        out = (query, key)[half]
        return pltpu.make_async_copy(
            staged.at[k, half, c], out.at[:, out_columns(k)], keep_sem.at[k, half]
        )

    def give(k, half):
        out = (query, key)[half]
        return remote(
            staged.at[k, half, 1 - c],
            out.at[:, out_columns(k)],
            give_send.at[k, half],
            give_recv.at[k, half],
            mate,
        )

    def norm_tokens():
        step = 64

        def body(i, carry):
            at = pl.ds(pl.multiple_of(i * step, step), step)
            wide = tokens[at, :].astype(jnp.float32)
            scale = lax.rsqrt(jnp.mean(wide * wide, axis=-1, keepdims=True) + 1e-06)
            normed[c, at, :] = (wide * scale * norm_gain[...]).astype(jnp.bfloat16)
            return carry

        lax.fori_loop(0, per_token // step, body, 0)
        tokens_to_mate().start()

    def sum_cores(k):
        for half in range(PAIR):
            load(k, half).wait()
            to_mate(k, half).wait_recv()
        pair_out[k] = (own_part[k, 1 - x] + core_part[k, 1 - x]).astype(jnp.bfloat16)
        to_across(k).start()

    def line_start(k):
        if k == line_last:
            last(k, z).wait_recv()

        @pl.when(z > 0)
        def _():
            along(k, z, 0).start()

        @pl.when(z < line - 1)
        def _():
            along(k, z, 1).start()

    def sum_pair(k):
        to_across(k).wait_recv()
        total = (own_part[k, x] + core_part[k, x] + pair_in[k].astype(jnp.float32)) / groups
        mean_out[k] = total
        here = pl.ds(k * block, block)
        teacher_out[k] = EMA_DECAY * teacher[:, here] + (1.0 - EMA_DECAY) * total
        weights[k, x, pl.ds(pl.multiple_of(f * rows, 16), rows), :] = total.astype(jnp.bfloat16)

        if k != line_last:
            line_start(k)
        first(k, z).start()
        for copy in stores(k):
            copy.start()

    def sides(t):
        yield z >= t, z - t, 1, z < line - 1
        yield z < line - t, z + t, 0, z > 0

    def line_step(k, t):
        for there, slab, way, onward in sides(t):

            @pl.when(there)
            def _():
                along(k, slab, way).wait_recv()

                @pl.when(onward)
                def _():
                    along(k, slab, way).start()

                if k != line_last:
                    first(k, slab).start()

    def plane_step(k, t):
        if t == 0:
            first(k, z).wait_recv()
            last(k, z).start()
            return
        for there, slab, way, onward in sides(t):

            @pl.when(there)
            def _():
                first(k, slab).wait_recv()
                last(k, slab).start()

    def arrived(k):
        for slab in range(line):
            last(k, slab).wait_recv()

    def project(k, half, core):
        step = 256 if per_token % 256 == 0 else per_token
        tile = 256 if block % 256 == 0 else HEAD
        gain = (query_gain, key_gain)[half][...]

        def body(i, carry):
            at = pl.ds(pl.multiple_of(i * step, step), step)
            for start in range(0, block, tile):
                made = jnp.dot(
                    normed[core, at, :],
                    weights[k, half, :, start : start + tile],
                    preferred_element_type=jnp.float32,
                )
                made = made * model_width ** (-0.5)
                for head in range(0, tile, HEAD):
                    one = made[:, head : head + HEAD]
                    scale = lax.rsqrt(jnp.mean(one * one, axis=-1, keepdims=True) + 1e-06)
                    staged[k, half, core, at, start + head : start + head + HEAD] = (
                        one * scale * gain
                    ).astype(jnp.bfloat16)
            return carry

        lax.fori_loop(0, per_token // step, body, 0)

    def project_other(k, half):
        project(k, half, 1 - c)
        give(k, half).start()

    def project_own(k, half):
        project(k, half, c)
        keep(k, half).start()

    for k in range(chunks):
        for half in range(PAIR):
            to_mate(k, half).start()
            load(k, half).start()
    norm_tokens()

    events = []
    period, hop = 25, 4
    for k in range(chunks):
        events.append((4 + k, functools.partial(sum_cores, k)))
        events.append((12 + 4 * k, functools.partial(sum_pair, k)))
        if k == line_last:
            events.append((18 + 4 * k, functools.partial(plane_step, k, 0)))
            events.append((12 + 12 * k, functools.partial(line_start, k)))
            for t in range(1, line):
                events.append((12 + 12 * k + 20 * t, functools.partial(line_step, k, t)))
            done = 33 + period * k
        else:
            for t in range(1, line):
                events.append((12 + 12 * k + hop * t, functools.partial(line_step, k, t)))
            for t in range(line):
                events.append((20 + period * k + 6 * t, functools.partial(plane_step, k, t)))
            done = 44 + period * (k + 1)
            events.append((done, functools.partial(arrived, k)))
        if k == 0:
            events.append((done, lambda: tokens_to_mate().wait_recv()))
        for half in range(PAIR):
            events.append((done + 6 * half, functools.partial(project_other, k, half)))
            events.append((done + 6 * half + 3, functools.partial(project_own, k, half)))
    for _, event in sorted(events, key=lambda item: item[0]):
        event()

    tokens_to_mate().wait_send()
    for k in range(chunks):
        to_across(k).wait_send()
        for half in range(PAIR):
            to_mate(k, half).wait_send()
            keep(k, half).wait()
            give(k, half).wait_send()
        for copy in stores(k):
            copy.wait()
        if k == line_last:
            first(k, z).wait_send()
            last(k, z).wait_send()
        for slab in range(line):
            if k != line_last:
                first(k, slab).wait_send()
                last(k, slab).wait_send()

            @pl.when((z > 0) & (z <= slab))
            def _():
                along(k, slab, 0).wait_send()

            @pl.when((z < line - 1) & (z >= slab))
            def _():
                along(k, slab, 1).wait_send()

    for k in range(chunks):
        for half in range(PAIR):
            give(k, half).wait_recv()


def shards(groups, members, tokens, student, teacher, norm_gain, query_gain, key_gain):
    per_token, model_width = tokens.shape
    rows, width = teacher.shape
    line = members // PAIR
    chunks = chunk_count(width, line)
    block = width // chunks
    dma = pltpu.SemaphoreType.DMA
    vmem = pl.BlockSpec(memory_space=pltpu.VMEM)
    hbm = pl.BlockSpec(memory_space=pl.ANY)
    f32, bf16 = jnp.float32, jnp.bfloat16
    return pl.pallas_call(
        functools.partial(kernel, groups, line, chunks),
        out_shape=(
            jax.ShapeDtypeStruct((rows, width), f32),
            jax.ShapeDtypeStruct((rows, width), f32),
            jax.ShapeDtypeStruct((per_token, model_width), bf16),
            jax.ShapeDtypeStruct((per_token, model_width), bf16),
        ),
        in_specs=[hbm, vmem, vmem, vmem, vmem, vmem],
        out_specs=(hbm, hbm, hbm, hbm),
        scratch_shapes=[
            pltpu.VMEM((chunks, PAIR, rows, block), f32),
            pltpu.VMEM((chunks, PAIR, rows, block), f32),
            pltpu.VMEM((chunks, rows, block), bf16),
            pltpu.VMEM((chunks, rows, block), bf16),
            pltpu.VMEM((chunks, PAIR, rows * members, block), bf16),
            pltpu.VMEM((PAIR, per_token, model_width), bf16),
            pltpu.VMEM((chunks, PAIR, PAIR, per_token, block), bf16),
            pltpu.VMEM((chunks, rows, block), f32),
            pltpu.VMEM((chunks, rows, block), f32),
            dma((chunks, PAIR)),
            dma((chunks, PAIR)),
            dma((chunks, PAIR)),
            dma((chunks,)),
            dma((chunks,)),
            dma((chunks, 2, line)),
            dma((chunks, line)),
            dma((chunks, line)),
            dma((chunks, line)),
            dma((chunks, line)),
            dma((chunks, line)),
            dma((2,)),
            dma((chunks, 2)),
            dma((chunks, PAIR)),
            dma((chunks, PAIR)),
            dma((chunks, PAIR)),
        ],
        compiler_params=pltpu.CompilerParams(
            collective_id=0, has_side_effects=True, vmem_limit_bytes=60 * 2**20
        ),
        cost_estimate=pl.CostEstimate(
            flops=4 * per_token * model_width * model_width,
            bytes_accessed=4 * student.size + 8 * tokens.size,
            transcendentals=0,
        ),
    )(
        student,
        tokens,
        teacher,
        norm_gain.reshape(1, -1),
        query_gain.reshape(1, -1),
        key_gain.reshape(1, -1),
    )


def solution(mesh):
    placed = (
        P(("group", "fsdp"), None),
        P("group", "fsdp", None),
        P("fsdp", "group"),
        P(),
        P(),
        P(),
    )
    return jax.shard_map(
        functools.partial(shards, mesh.shape["group"], mesh.shape["fsdp"]),
        mesh=mesh,
        in_specs=placed,
        out_specs=(
            P("fsdp", "group"),
            P("fsdp", "group"),
            P(("group", "fsdp"), None),
            P(("group", "fsdp"), None),
        ),
        check_vma=False,
    )
```
